256 devices in a mesh: group: 32 (over x, y, core), tensor: 8 (over z).
Axes of the slice: x: 4, y: 4, z: 8, core: 2. Of those that a mesh axis runs over, the one named last changes fastest.
Arguments:
- tokens: bfloat16 [65536, 8192], P('group', 'tensor'), may hold values from -6 to 6
- kv_weight: bfloat16 [8192, 2048], P('tensor'), may hold values from -0.0625 to 0.0625
- a_pool: bfloat16 [64, 8192, 128], P('group', 'tensor'), may hold values from -0.0625 to 0.0625
- b_pool: bfloat16 [64, 64, 2048], P('group', None, 'tensor'), may hold values from -0.75 to 0.75
- request_entry: int32 [448], P('group'), may hold values from 0 to 14, as said below
- block_request: int32 [32, 16], P('group'), may hold values from 0 to 13, never falling along the last dimension, each value on 1 to 2 neighbouring positions
- fetch_source: int32 [416, 1], P('group'), may hold values from 0 to 31; in each aligned block of 13 rows (0 to 12, 13 to 25, ...) no two rows name the same one
- fetch_slot: int32 [416], P('group'), may hold values from 0 to 1
Outputs:
- keys_values: bfloat16 [2048, 65536], P('tensor', 'group')
The draws below stay inside these ranges and needn't reach their ends.
Inputs may be any that keep to these rules, and one draw needn't show every extreme that they name: Request r of group g uses entry request_entry[g * 14 + r] of the group's working table: entries below 2 are the group's own pool slots, entry 2 + f is the adapter of the group's f-th fetch; every fetch of a group is used by some request of it. `block_request`: requests cover whole blocks in order, each 1 to 2 blocks, some request exactly that many. The f-th fetch of group g reads slot fetch_slot[g * 13 + f] of the pool of group fetch_source[g * 13 + f, 0], which may be g itself; no group has more than 1 fetches from one source group, and some group has exactly 1.
All inputs are finite; a program needn't handle non-finite values.
Results may differ from the reference program's by a relative error of at most 0.02.
Values may be sent and summed in bfloat16 or wider, within the bound.
No kernel may reach another device: no remote copies, remote signals or barrier semaphores. Data moves between devices by JAX's collectives and lax.ppermute only.
A program may use at most 128 MiB of HBM per device.

```python
import math
import jax
import jax.numpy as jnp
import numpy as np
from jax import lax

D = 8192
KVH = 8
HEAD = 128
RANK = 64
BLK = 128
BLOCKS = 16
REQ = 14
POOL = 2
CAP = 1
FETCH = 13
GROUPS = 32
BATCH_LINE_COUNT = 2048
TOKENS = 65536
ATTENTION_FEATS = 2048
ADAPTERS = 64
N_GROUP = 32
N_TENSOR = 8


def draw_request_entry(key, part):
    key = jax.random.fold_in(key, 7)

    def one_group(group_key):
        first_key, second_key, third_key = jax.random.split(group_key, 3)
        fetched = POOL + jax.random.permutation(first_key, FETCH).astype(jnp.int32)
        others = jax.random.randint(second_key, (REQ - FETCH,), 0, POOL + FETCH, dtype=jnp.int32)
        return jax.random.permutation(third_key, jnp.concatenate([fetched, others]))
    return jax.vmap(one_group)(jax.random.split(key, GROUPS)).reshape(-1).astype(jnp.int32)


def place_ends(values, key, smallest, high):
    index_at = [jax.random.randint(jax.random.fold_in(key, axis), (), 0, length) for axis, length in enumerate(values.shape)]
    widest = values.shape.index(max(values.shape))
    next_to = index_at[:widest] + [(index_at[widest] + 1) % values.shape[widest]] + index_at[widest + 1:]
    return values.at[tuple(index_at)].set(smallest).at[tuple(next_to)].set(high)


def steps_of(own_key, shape, cuts, least, high):
    def one(axis_at, parts):
        steps = jax.random.uniform(jax.random.fold_in(jax.random.fold_in(own_key, 6), axis_at), (parts,), jnp.float32, least / len(cuts), high / len(cuts))
        return jnp.repeat(jnp.exp(steps), shape[axis_at] // parts).reshape((-1,) + (1,) * (len(shape) - axis_at - 1))

    gain = one(*cuts[0])
    for cut in cuts[1:]:
        gain = gain * one(*cut)
    return gain


def profile(count, total, most, lean):
    loads = [(1 << 20) // math.isqrt(standing ** lean) + 1 for standing in range(2, count + 1)]
    rest, counts = total - most - (count - 1), [1] * (count - 1)
    while rest > 0:
        free = [i for i in range(count - 1) if counts[i] < most]
        pool, budget = sum([loads[i] for i in free]), rest
        for i in free:
            addition = min(most - counts[i], max(1, budget * loads[i] // pool), rest)
            counts[i] = counts[i] + addition
            rest = rest - addition
    return np.array([most] + counts)


def ragged(stream_key, number_of, total, limit, skew):
    if number_of == 2:
        one = jax.random.randint(stream_key, (), max(1, total - limit), min(limit, total - 1) + 1)
        return jnp.stack([one, total - one])
    tallies = jnp.asarray(profile(number_of, total, limit, skew), jnp.int32)
    couples = (number_of - 1) // 2
    giver, taker = tallies[1:1 + 2 * couples:2], tallies[2:2 + 2 * couples:2]
    room = jnp.minimum(giver - 1, limit - taker)
    passed = jax.random.randint(jax.random.fold_in(stream_key, 1), (couples,), 0, 1 << 20) % (room + 1)
    tallies = tallies.at[1:1 + 2 * couples:2].set(giver - passed).at[2:2 + 2 * couples:2].set(taker + passed)
    return tallies[jax.random.permutation(jax.random.fold_in(stream_key, 2), number_of)]


def assign_block(stream_key, own, number, rows, amount, top, reach, lean):
    order = jax.random.permutation(stream_key, amount)
    packed, ordinary = load_shares(amount, rows * top, reach, lean, True), load_shares(amount, rows * top, reach, lean, False)
    places = jnp.arange(amount)

    def named(tallies, turn):
        used = int((tallies > 0).sum())
        fixed = max(1, used // 4)
        shifted = fixed + (places - fixed + turn * (used - fixed)) % max(1, amount - fixed)
        return jnp.zeros((amount,), jnp.int32).at[order[jnp.where(places < fixed, places, shifted)]].set(jnp.asarray(tallies, jnp.int32))

    tallies = jnp.where(number % 4 == 0, named(packed, number // 4), named(ordinary, number - number // 4 - 1))
    mixed = jax.random.permutation(jax.random.fold_in(own, 3), amount)
    donor, sink = mixed[0:amount // 2 * 2:2], mixed[1:amount // 2 * 2:2]
    margin = jnp.minimum(tallies[donor] - 1, reach - tallies[sink]) // 2
    margin = jnp.where((donor == order[0]) | (sink == order[0]) | (tallies[sink] == 0), 0, jnp.maximum(margin, 0))
    shifted = jax.random.randint(jax.random.fold_in(own, 4), (amount // 2,), 0, 1 << 20) % (margin + 1)
    tallies = tallies.at[donor].add(-shifted).at[sink].add(shifted)
    items = jnp.searchsorted(jnp.cumsum(tallies), jnp.arange(rows * top), side="right").astype(jnp.int32)
    grid = items.reshape(top, rows).T
    grid = grid[jax.random.permutation(jax.random.fold_in(own, 1), rows)]
    turn = jax.random.randint(jax.random.fold_in(own, 2), (rows, 1), 0, top)
    return jnp.take_along_axis(grid, (jnp.arange(top)[None, :] + turn) % top, axis=1)


def load_shares(amount, total, most, lean, full):
    weights = [(1 << 20) // math.isqrt(standing ** lean) + 1 for standing in range(1, amount + 1)]
    largest = most if full else min(most, max(-(-total // amount), total * weights[0] // sum(weights)))
    least = 1 if total - largest >= amount - 1 else 0
    counts, rest = [largest] + [least] * (amount - 1), total - largest - least * (amount - 1)
    while rest > 0:
        movable = [i for i in range(1, amount) if counts[i] < largest] or [i for i in range(1, amount) if counts[i] < most]
        pool, remaining = sum([weights[i] for i in movable]), rest
        for i in movable:
            addition = min(most - counts[i], max(1, remaining * weights[i] // pool), rest)
            counts[i] = counts[i] + addition
            rest = rest - addition
    return np.array(counts)


def bell_draw(own_key, dims, scale, limit, pieces=(), kind=jnp.bfloat16):
    level = steps_of(own_key, dims, pieces, -0.22, 0.18) if pieces else 1.0
    array = jax.random.normal(own_key, dims, jnp.float32) * scale * level
    return jnp.minimum(jnp.maximum(array, -limit), limit).astype(kind)


def setup_inputs(seed: int = 0) -> dict:
    seeds = jax.random.split(jax.random.key(seed), 9)
    tokens = bell_draw(seeds[0], (TOKENS, D), 1.0, 6.0, ((0, 32), (1, 8)))
    kv_weight = bell_draw(seeds[1], (D, ATTENTION_FEATS), D ** -0.5, 0.0625, ((0, 8),))
    a_pool = bell_draw(seeds[2], (ADAPTERS, D, 2 * RANK), D ** -0.5, 0.0625, ((0, 32), (1, 8)))
    b_pool = bell_draw(seeds[3], (ADAPTERS, RANK, ATTENTION_FEATS), RANK ** -0.5, 0.75, ((0, 32), (2, 8)))
    request_entry = draw_request_entry(jax.random.fold_in(seeds[8], 71), 0)
    block_request = jax.vmap(lambda own: jnp.searchsorted(jnp.cumsum(ragged(own, REQ, BLOCKS, (BLOCKS - REQ) // 2 + 1, 2)), jnp.arange(BLOCKS), side="right"))(jax.random.split(seeds[5], GROUPS)).reshape((GROUPS, BLOCKS)).astype(jnp.int32)
    fetch_source_keys = jax.random.split(jax.random.fold_in(seeds[6], 1), (GROUPS * FETCH) // FETCH)
    fetch_source_turns = jax.random.permutation(jax.random.fold_in(seeds[6], 3), (GROUPS * FETCH) // FETCH)
    fetch_source = jax.vmap(lambda own, number: assign_block(jax.random.fold_in(seeds[6], 2), own, number, FETCH, N_GROUP, 1, CAP, 2))(fetch_source_keys, fetch_source_turns).reshape((GROUPS * FETCH, 1))
    fetch_slot = place_ends(jax.random.randint(seeds[7], (GROUPS * FETCH,), 0, POOL), jax.random.fold_in(seeds[7], 1), 0, POOL - 1).astype(jnp.int32)
    return {"tokens": tokens, "kv_weight": kv_weight, "a_pool": a_pool, "b_pool": b_pool, "request_entry": request_entry, "block_request": block_request, "fetch_source": fetch_source, "fetch_slot": fetch_slot}


def adapter_table(request_entry, fetch_source, fetch_slot):
    entries = request_entry.reshape(GROUPS, REQ)
    owners = fetch_source[:, 0].reshape(GROUPS, FETCH)
    slot_ids = fetch_slot.reshape(GROUPS, FETCH)
    fetched = owners * POOL + slot_ids
    group_ids = jnp.arange(GROUPS, dtype=jnp.int32)[:, None]
    resident = group_ids * POOL + entries
    fetch_pos = jnp.clip(entries - POOL, 0, FETCH - 1).astype(jnp.int32)
    remote = jnp.take_along_axis(fetched, fetch_pos, axis=1)
    return jnp.where(entries < POOL, resident, remote).astype(jnp.int32)


def reference(tokens, kv_weight, a_pool, b_pool, request_entry, block_request, fetch_source, fetch_slot):
    adapter_of = adapter_table(request_entry, fetch_source, fetch_slot)
    block_adapter = jnp.take_along_axis(adapter_of, block_request, axis=1).astype(jnp.int32)
    weights = kv_weight.reshape(N_TENSOR, D // N_TENSOR, ATTENTION_FEATS).astype(jnp.float32)

    def one_group(group_data):
        group_tokens, adapters = group_data
        slices = group_tokens.reshape(BATCH_LINE_COUNT, N_TENSOR, D // N_TENSOR).astype(jnp.float32)
        partials = jnp.einsum("tkd,kdc->ktc", slices, weights)
        rounded = lax.optimization_barrier(partials.astype(jnp.bfloat16))
        pretrained_output_total = jnp.sum(rounded.astype(jnp.float32), axis=0)
        a_blocks = a_pool[adapters].astype(jnp.float32)
        x_blocks = group_tokens.reshape(BLOCKS, BLK, D).astype(jnp.float32)
        shrink = jnp.einsum("btd,bdr->btr", x_blocks, a_blocks).astype(jnp.bfloat16)
        lifting_factor_tiles = b_pool[adapters].astype(jnp.float32).reshape(BLOCKS, RANK, KVH, 2, HEAD)
        bottleneck_partial_terms = shrink.astype(jnp.float32).reshape(BLOCKS, BLK, 2, RANK)
        adapter_correction = jnp.einsum("kdfe,kerft->rftkd", bottleneck_partial_terms, lifting_factor_tiles).reshape(ATTENTION_FEATS, BATCH_LINE_COUNT)
        return (pretrained_output_total.T + adapter_correction).astype(jnp.bfloat16)

    outputs = lax.map(one_group, (tokens.reshape(GROUPS, BATCH_LINE_COUNT, D), block_adapter))
    return jnp.moveaxis(outputs, 0, 1).reshape(ATTENTION_FEATS, TOKENS)
```

```python
import functools

import jax
import jax.numpy as jnp
from jax import lax
from jax.experimental import pallas as pl
from jax.experimental.pallas import tpu as pltpu
from jax.sharding import PartitionSpec as P

HEAD = 128
SIDE = 4
CORES = 2
LANES = 128
NT = (((1,), (1,)), ((), ()))


def base_kernel(tokens_ref, weight_ref, out_ref):
    rows = tokens_ref.shape[0]
    tile = 512

    @pl.loop(0, rows // tile)
    def _(i):
        at = pl.ds(pl.multiple_of(i * tile, tile), tile)
        out_ref[0, at, :] = jnp.dot(
            tokens_ref[at, :], weight_ref[...], preferred_element_type=jnp.float32
        ).astype(out_ref.dtype)


def base_partial(tokens, kv_weight, parts):
    rows, depth = tokens.shape
    columns = kv_weight.shape[1] // parts
    return pl.pallas_call(
        base_kernel,
        grid=(parts,),
        in_specs=[
            pl.BlockSpec((rows, depth), lambda d: (0, 0)),
            pl.BlockSpec((depth, columns), lambda d: (0, d)),
        ],
        out_specs=pl.BlockSpec((1, rows, columns), lambda d: (d, 0, 0)),
        out_shape=jax.ShapeDtypeStruct((parts, rows, columns), jnp.bfloat16),
        cost_estimate=pl.CostEstimate(
            flops=2 * rows * depth * columns * parts,
            bytes_accessed=2 * (rows * depth + depth * columns * parts + rows * columns * parts),
            transcendentals=0,
        ),
        compiler_params=pltpu.CompilerParams(vmem_limit_bytes=40 * 2**20),
        name="base_partial",
    )(tokens, kv_weight)


def shrink_kernel(
    requests, blocks, fetches, pool, table_ref, place_ref, own_tokens, sib_tokens, *refs
):
    first, second = refs[0:5], refs[5:10]
    own_out, sib_out, token_buf, factor_buf, token_sem, factor_sem = refs[10:]
    tile = token_buf.shape[1]
    depth = token_buf.shape[2]
    half = depth // 2
    x, y, core = place_ref[0], place_ref[1], place_ref[2]

    def lookup(who, b):
        request = table_ref[who, requests + b]
        entry = table_ref[who, request]
        fetch = jnp.clip(entry - pool, 0, fetches - 1)
        source = table_ref[who, requests + blocks + fetch]
        slot = table_ref[who, requests + blocks + fetches + fetch]
        mine = entry < pool
        own_group = (x * SIDE + y) * CORES + jnp.where(who == 0, core, 1 - core)
        source = jnp.where(mine, own_group, source)
        slot = jnp.where(mine, entry, slot)
        relative_x = lax.rem(source // (SIDE * CORES) - x + SIDE, SIDE)
        relative_y = lax.rem(lax.rem(source // CORES, SIDE) - y + SIDE, SIDE)
        return lax.rem(source, CORES) == core, relative_x, relative_y, slot

    def offset(relative, slot):
        return jnp.where(
            relative == 0, 0, jnp.where(relative == 3, 2, jnp.where(relative == 1, 4, 6))
        ) + slot

    def start_half(pieces, which, at, relative, index):
        def copy(piece, entry):
            pltpu.make_async_copy(
                pieces[piece].at[entry], factor_buf.at[at, which], factor_sem.at[at, which]
            ).start()

        pl.when(relative == 0)(lambda: copy(0, index))
        pl.when(relative == 3)(lambda: copy(1, index))
        pl.when(relative == 1)(lambda: copy(2, index))
        pl.when((relative == 2) & (index < 4))(lambda: copy(3, index))
        pl.when((relative == 2) & (index >= 4))(lambda: copy(4, index - 4))

    for who, tokens_ref in ((0, own_tokens), (1, sib_tokens)):

        @pl.loop(0, blocks)
        def _(b):
            active, relative_x, relative_y, slot = lookup(who, b)
            at = who * blocks + b

            @pl.when(active)
            def _():
                pltpu.make_async_copy(
                    tokens_ref.at[pl.ds(pl.multiple_of(b * tile, tile), tile)],
                    token_buf.at[at],
                    token_sem.at[at],
                ).start()
                start_half(first, 0, at, relative_x, offset(relative_y, slot))
                start_half(second, 1, at, relative_y, offset(relative_x, slot))

    for who, out_ref in ((0, own_out), (1, sib_out)):

        @pl.loop(0, blocks)
        def _(b):
            active = lookup(who, b)[0]
            at = who * blocks + b

            @pl.when(active)
            def _():
                pltpu.make_async_copy(
                    own_tokens.at[pl.ds(0, tile)], token_buf.at[at], token_sem.at[at]
                ).wait()
                for which in range(2):
                    pltpu.make_async_copy(
                        first[0].at[0], factor_buf.at[at, which], factor_sem.at[at, which]
                    ).wait()
                total = jnp.dot(
                    token_buf[at, :, :half],
                    factor_buf[at, 0, :half],
                    preferred_element_type=jnp.float32,
                ) + jnp.dot(
                    token_buf[at, :, half:],
                    factor_buf[at, 1, :half],
                    preferred_element_type=jnp.float32,
                )
                out_ref[b, :tile] = total.astype(out_ref.dtype)
                out_ref[b, tile : tile + 64] = factor_buf[at, 0, half:]
                out_ref[b, tile + 64 :] = factor_buf[at, 1, half:]

            @pl.when(jnp.logical_not(active))
            def _():
                out_ref[b] = jnp.zeros(out_ref.shape[1:], out_ref.dtype)


def partial_shrink(table, place, own_tokens, sib_tokens, first, second, sizes):
    requests, blocks, fetches, pool = sizes
    rows, depth = own_tokens.shape
    tile = rows // blocks
    height = first[0].shape[1]
    smem = pl.BlockSpec(memory_space=pltpu.SMEM)
    hbm = pl.BlockSpec(memory_space=pl.ANY)
    shape = jax.ShapeDtypeStruct((blocks, tile + 2 * (height - depth // 2), LANES), jnp.bfloat16)
    return pl.pallas_call(
        functools.partial(shrink_kernel, requests, blocks, fetches, pool),
        in_specs=[smem, smem] + [hbm] * 12,
        out_specs=[pl.BlockSpec(memory_space=pltpu.VMEM)] * 2,
        out_shape=[shape, shape],
        scratch_shapes=[
            pltpu.VMEM((2 * blocks, tile, depth), jnp.bfloat16),
            pltpu.VMEM((2 * blocks, 2, height, LANES), jnp.bfloat16),
            pltpu.SemaphoreType.DMA((2 * blocks,)),
            pltpu.SemaphoreType.DMA((2 * blocks, 2)),
        ],
        cost_estimate=pl.CostEstimate(
            flops=2 * rows * depth * LANES, bytes_accessed=12 * 2**20, transcendentals=0
        ),
        compiler_params=pltpu.CompilerParams(vmem_limit_bytes=40 * 2**20),
        name="partial_shrink",
    )(table, place, own_tokens, sib_tokens, *first, *second)


def finish_kernel(base_ref, shrink_ref, lift_ref, out_ref):
    tile = lift_ref.shape[1]
    blocks = lift_ref.shape[0]
    columns = base_ref.shape[1]
    rank = tile // 2
    line = lax.broadcasted_iota(jnp.int32, (columns, columns), 0)
    lane = lax.broadcasted_iota(jnp.int32, (columns, columns), 1)
    eye = jnp.where(line == lane, 1.0, 0.0).astype(jnp.bfloat16)
    for b in range(blocks):
        at = pl.ds(b * tile, tile)
        turned = lax.dot_general(eye, base_ref[at, :], NT, preferred_element_type=jnp.float32)
        for kind in range(2):
            delta = lax.dot_general(
                lift_ref[b, kind * rank : (kind + 1) * rank],
                shrink_ref[at, kind * rank : (kind + 1) * rank],
                (((0,), (1,)), ((), ())),
                preferred_element_type=jnp.float32,
            )
            rows = slice(kind * HEAD, (kind + 1) * HEAD)
            out_ref[rows, at] = (turned[rows] + delta).astype(out_ref.dtype)


def finish(base, shrink, lift):
    rows, columns = base.shape
    parts = 2
    step, lifts = rows // parts, lift.shape[0] // parts
    return pl.pallas_call(
        finish_kernel,
        grid=(parts,),
        in_specs=[
            pl.BlockSpec((step, columns), lambda i: (i, 0)),
            pl.BlockSpec((step, shrink.shape[1]), lambda i: (i, 0)),
            pl.BlockSpec((lifts,) + lift.shape[1:], lambda i: (i, 0, 0)),
        ],
        out_specs=pl.BlockSpec((columns, step), lambda i: (0, i)),
        out_shape=jax.ShapeDtypeStruct((columns, rows), jnp.bfloat16),
        cost_estimate=pl.CostEstimate(
            flops=2 * rows * columns * (columns + LANES),
            bytes_accessed=6 * rows * columns,
            transcendentals=0,
        ),
        compiler_params=pltpu.CompilerParams(vmem_limit_bytes=40 * 2**20),
        name="finish",
    )(base, shrink, lift)


def moves():
    def index(x, y, core):
        return ((x % SIDE) * SIDE + y % SIDE) * CORES + core

    places = [
        (x, y, core) for x in range(SIDE) for y in range(SIDE) for core in range(CORES)
    ]

    def shift(dx, dy):
        return [(index(x, y, c), index(x + dx, y + dy, c)) for x, y, c in places]

    swap = [(index(x, y, c), index(x, y, 1 - c)) for x, y, c in places]
    return (shift(1, 0), shift(-1, 0)), (shift(0, 1), shift(0, -1)), swap


def per_device(
    tokens, kv_weight, a_pool, b_pool, request_entry, block_request, fetch_source, fetch_slot
):
    tensor = lax.axis_size("tensor")
    rows, depth = tokens.shape
    blocks = block_request.shape[1]
    pool = a_pool.shape[0]
    half = depth // 2
    along_x, along_y, swap = moves()

    partial = base_partial(tokens, kv_weight, tensor)
    base = lax.psum_scatter(
        partial.reshape(tensor * rows, -1), "tensor", scatter_dimension=0, tiled=True
    )

    position = lax.axis_index("group")
    place = jnp.stack(
        [position // (SIDE * CORES), position // CORES % SIDE, position % CORES]
    ).astype(jnp.int32)
    table = jnp.concatenate(
        [request_entry, block_request[0], fetch_source[:, 0], fetch_slot]
    )
    table = jnp.stack([table, lax.ppermute(table, "group", swap)])
    sib_tokens = lax.ppermute(tokens, "group", swap)

    halves = (
        jnp.concatenate([a_pool[:, :half], b_pool[:, :, :HEAD]], axis=1),
        jnp.concatenate([a_pool[:, half:], b_pool[:, :, HEAD:]], axis=1),
    )
    orders = ((along_y, along_x), (along_x, along_y))

    def send(value, way):
        return lax.ppermute(value, "group", way)

    lines = []
    for held, (line, _) in zip(halves, orders):
        up, down = send(held, line[0]), send(held, line[1])
        lines.append((held, up, down))
    gathered = []
    for (held, up, down), (line, _) in zip(lines, orders):
        far_up, far_down = send(up[:1], line[0]), send(down[1:], line[1])
        gathered.append(jnp.concatenate([held, up, down, far_up, far_down], axis=0))
    near = [
        (line, send(line, other[0]), send(line, other[1]))
        for line, (_, other) in zip(gathered, orders)
    ]
    first, second = [
        (line, up, down, send(up[: 2 * pool], other[0]), send(down[2 * pool :], other[1]))
        for (line, up, down), (_, other) in zip(near, orders)
    ]

    sizes = (request_entry.shape[0], blocks, fetch_slot.shape[0], pool)
    own, sib = partial_shrink(table, place, tokens, sib_tokens, first, second, sizes)
    both = own + lax.ppermute(sib, "group", swap)
    tile = rows // blocks
    shrink = both[:, :tile].reshape(rows, LANES)
    lift = both[:, tile:]

    shrink = lax.all_to_all(shrink, "tensor", split_axis=0, concat_axis=0, tiled=True)
    shrink = jnp.sum(
        shrink.reshape(tensor, rows // tensor, LANES).astype(jnp.float32), axis=0
    ).astype(jnp.bfloat16)
    shrink = jnp.broadcast_to(shrink[None], (tensor,) + shrink.shape).reshape(rows, LANES)
    shrink = lax.all_to_all(shrink, "tensor", split_axis=0, concat_axis=0, tiled=True)
    return finish(base, shrink, lift)


def solution(mesh):
    placed = (
        P("group", "tensor"),
        P("tensor", None),
        P("group", "tensor", None),
        P("group", None, "tensor"),
        P("group"),
        P("group", None),
        P("group", None),
        P("group"),
    )
    return jax.shard_map(
        per_device, mesh=mesh, in_specs=placed, out_specs=P("tensor", "group"), check_vma=False
    )
```

```python
import functools

import jax
import jax.numpy as jnp
from jax import lax
from jax.experimental import pallas as pl
from jax.experimental.pallas import tpu as pltpu
from jax.sharding import PartitionSpec as P

HEAD = 128
TILE = 512
VMEM = 60 * 2**20
NT = (((1,), (1,)), ((), ()))


def product_kernel(arrived, owner_ref, tokens_ref, weight_ref, *refs):
    outs = refs[-10:-8]
    token_buf, weight_buf, arrived_buf, out_buf = refs[-8:-4]
    token_sems, weight_sems, arrived_sems, out_sems = refs[-4:]
    columns = outs[0].shape[1]
    tiles = token_buf.shape[0]
    each = tiles // 2

    def token_copy(i):
        return pltpu.make_async_copy(
            tokens_ref.at[pl.ds(i * TILE, TILE)], token_buf.at[i], token_sems.at[i]
        )

    def weight_copy(which):
        at = pl.ds(pl.multiple_of(owner_ref[which] * columns, columns), columns)
        return pltpu.make_async_copy(
            weight_ref.at[:, at], weight_buf.at[which], weight_sems.at[which]
        )

    def arrived_copy(which):
        return pltpu.make_async_copy(refs[which], arrived_buf.at[which], arrived_sems.at[which])

    def out_copy(which):
        return pltpu.make_async_copy(out_buf.at[which], outs[which], out_sems.at[which])

    def fetch(i):
        which = i // each
        token_copy(i).start()
        if i % each == 0:
            weight_copy(which).start()
            if arrived:
                arrived_copy(which).start()

    ahead = 2
    for i in range(ahead):
        fetch(i)
    for i in range(tiles):
        which = i // each
        token_copy(i).wait()
        if i % each == 0:
            weight_copy(which).wait()
            if arrived:
                arrived_copy(which).wait()
        if i + ahead < tiles:
            fetch(i + ahead)
        rows = slice(i % each * TILE, (i % each + 1) * TILE)
        total = jnp.dot(token_buf[i], weight_buf[which], preferred_element_type=jnp.float32)
        if arrived:
            total += arrived_buf[which, rows, :].astype(jnp.float32)
        out_buf[which, rows, :] = total.astype(out_buf.dtype)
        if i % each == each - 1:
            out_copy(which).start()
    for which in range(2):
        out_copy(which).wait()


def product(tokens, kv_weight, owners, columns, arrived=(), after=()):
    rows, depth = tokens.shape
    hbm = pl.BlockSpec(memory_space=pl.ANY)
    return pl.pallas_call(
        functools.partial(product_kernel, len(arrived)),
        in_specs=[pl.BlockSpec(memory_space=pltpu.SMEM)] + [hbm] * (2 + len(arrived) + len(after)),
        out_specs=[hbm] * 2,
        out_shape=[jax.ShapeDtypeStruct((rows // 2, columns), jnp.bfloat16)] * 2,
        scratch_shapes=[
            pltpu.VMEM((rows // TILE, TILE, depth), jnp.bfloat16),
            pltpu.VMEM((2, depth, columns), jnp.bfloat16),
            pltpu.VMEM((2, rows // 2, columns), jnp.bfloat16),
            pltpu.VMEM((2, rows // 2, columns), jnp.bfloat16),
            pltpu.SemaphoreType.DMA((rows // TILE,)),
            pltpu.SemaphoreType.DMA((2,)),
            pltpu.SemaphoreType.DMA((2,)),
            pltpu.SemaphoreType.DMA((2,)),
        ],
        cost_estimate=pl.CostEstimate(
            flops=2 * rows * depth * columns,
            bytes_accessed=2 * (rows * depth + (2 * depth + rows) * columns),
            transcendentals=0,
        ),
        compiler_params=pltpu.CompilerParams(vmem_limit_bytes=VMEM),
        name="product",
    )(owners, tokens, kv_weight, *arrived, *after)


def shrink_kernel(
    adapter_ref, tokens_ref, pool_ref, first_ref, second_ref, out_ref, token_buf, factor_buf, sems
):
    del first_ref, second_ref
    blocks, tile, _ = token_buf.shape

    def copies(b):
        at = pl.ds(pl.multiple_of(b * tile, tile), tile)
        return (
            pltpu.make_async_copy(tokens_ref.at[at], token_buf.at[b], sems.at[b, 0]),
            pltpu.make_async_copy(
                pool_ref.at[adapter_ref[b], pl.ds(0, token_buf.shape[2])],
                factor_buf.at[b],
                sems.at[b, 1],
            ),
        )

    for b in range(blocks):
        for copy in copies(b):
            copy.start()
    for b in range(blocks):
        for copy in copies(b):
            copy.wait()
        out_ref[b * tile : (b + 1) * tile, :] = jnp.dot(
            token_buf[b], factor_buf[b], preferred_element_type=jnp.float32
        ).astype(out_ref.dtype)


def partial_shrink(adapters, tokens, pools, after):
    blocks = adapters.shape[0]
    rows, depth = tokens.shape
    width = pools.shape[2]
    return pl.pallas_call(
        shrink_kernel,
        in_specs=[pl.BlockSpec(memory_space=pltpu.SMEM)]
        + [pl.BlockSpec(memory_space=pl.ANY)] * 4,
        out_specs=pl.BlockSpec(memory_space=pltpu.VMEM),
        out_shape=jax.ShapeDtypeStruct((rows, width), jnp.bfloat16),
        scratch_shapes=[
            pltpu.VMEM((blocks, rows // blocks, depth), jnp.bfloat16),
            pltpu.VMEM((blocks, depth, width), jnp.bfloat16),
            pltpu.SemaphoreType.DMA((blocks, 2)),
        ],
        cost_estimate=pl.CostEstimate(
            flops=2 * rows * depth * width,
            bytes_accessed=2 * (rows + blocks * width) * depth,
            transcendentals=0,
        ),
        compiler_params=pltpu.CompilerParams(vmem_limit_bytes=VMEM),
        name="partial_shrink",
    )(adapters, tokens, pools, *after)


def turn_kernel(adapter_ref, *refs):
    sums, pool_ref, out_ref, lift_ref, sems = refs[:4], *refs[4:]
    height = lift_ref.shape[1]
    first = pool_ref.shape[1] - height
    columns = out_ref.shape[0]
    half = out_ref.shape[1] // 2

    def copy(b):
        return pltpu.make_async_copy(
            pool_ref.at[adapter_ref[b], pl.ds(first, height)], lift_ref.at[b], sems.at[b]
        )

    for b in range(lift_ref.shape[0]):
        copy(b).start()
    line = lax.broadcasted_iota(jnp.int32, (columns, columns), 0)
    lane = lax.broadcasted_iota(jnp.int32, (columns, columns), 1)
    eye = jnp.where(line == lane, 1.0, 0.0).astype(jnp.bfloat16)
    for which in range(2):
        for start in range(0, half, TILE):
            at = slice(start, start + TILE)
            total = add(sums[2 * which][at, :], sums[2 * which + 1][at, :])
            out_ref[:, which * half + start : which * half + start + TILE] = lax.dot_general(
                eye, total, NT, preferred_element_type=jnp.float32
            ).astype(out_ref.dtype)
    for b in range(lift_ref.shape[0]):
        copy(b).wait()


def turn(adapters, sums, pools, height):
    rows, columns = 2 * sums[0].shape[0], sums[0].shape[1]
    blocks = adapters.shape[0]
    vmem = pl.BlockSpec(memory_space=pltpu.VMEM)
    return pl.pallas_call(
        turn_kernel,
        in_specs=[pl.BlockSpec(memory_space=pltpu.SMEM)]
        + [vmem] * 4
        + [pl.BlockSpec(memory_space=pl.ANY)],
        out_specs=[vmem] * 2,
        out_shape=[
            jax.ShapeDtypeStruct((columns, rows), jnp.bfloat16),
            jax.ShapeDtypeStruct((blocks, height, pools.shape[2]), jnp.bfloat16),
        ],
        scratch_shapes=[pltpu.SemaphoreType.DMA((blocks,))],
        cost_estimate=pl.CostEstimate(
            flops=2 * rows * columns * columns, bytes_accessed=6 * rows * columns, transcendentals=0
        ),
        compiler_params=pltpu.CompilerParams(vmem_limit_bytes=VMEM),
        name="turn",
    )(adapters, *sums, pools)


def finish_kernel(base_ref, shrink_ref, lift_ref, out_ref):
    blocks, height, _ = lift_ref.shape
    rank = height // 2
    tile = base_ref.shape[1] // blocks
    for b in range(blocks):
        at = slice(b * tile, (b + 1) * tile)
        for kind in range(2):
            rows = slice(kind * HEAD, (kind + 1) * HEAD)
            ranks = slice(kind * rank, (kind + 1) * rank)
            delta = lax.dot_general(
                lift_ref[b, ranks, :],
                shrink_ref[at, ranks],
                (((0,), (1,)), ((), ())),
                preferred_element_type=jnp.float32,
            )
            out_ref[rows, at] = (base_ref[rows, at].astype(jnp.float32) + delta).astype(
                out_ref.dtype
            )


def finish(base, shrink, lift):
    columns, rows = base.shape
    steps = 2
    step, lifts = rows // steps, lift.shape[0] // steps
    return pl.pallas_call(
        finish_kernel,
        grid=(steps,),
        in_specs=[
            pl.BlockSpec((columns, step), lambda i: (0, i)),
            pl.BlockSpec((step, shrink.shape[1]), lambda i: (i, 0)),
            pl.BlockSpec((lifts,) + lift.shape[1:], lambda i: (i, 0, 0)),
        ],
        out_specs=pl.BlockSpec((columns, step), lambda i: (0, i)),
        out_shape=jax.ShapeDtypeStruct((columns, rows), jnp.bfloat16),
        cost_estimate=pl.CostEstimate(
            flops=2 * rows * columns * HEAD, bytes_accessed=6 * rows * columns, transcendentals=0
        ),
        compiler_params=pltpu.CompilerParams(vmem_limit_bytes=VMEM),
        name="finish",
    )(base, shrink, lift)


def add(*terms):
    return sum(term.astype(jnp.float32) for term in terms).astype(jnp.bfloat16)


def ring_sum(tokens, kv_weight, between):
    count = lax.axis_size("tensor")
    me = lax.axis_index("tensor")
    far = count // 2

    def hop(value, way):
        return lax.ppermute(value, "tensor", [(i, (i + way) % count) for i in range(count)])

    ways = (1, -1)
    columns = kv_weight.shape[1] // count

    def at(shift, arrived=(), after=()):
        owners = (me + jnp.array([way * shift for way in ways], jnp.int32) + count) % count
        return product(tokens, kv_weight, owners, columns, arrived, after)

    long = at(far)
    short = at(1 - far, after=long[:1])
    for step in range(1, far):
        long = at(far - step, [hop(value, way) for value, way in zip(long, ways)], short[:1])
        arrived = [hop(value, -way) for value, way in zip(short, ways)]
        after = long[0]
        if step == far - 1:
            last = [hop(value, way) for value, way in zip(long, ways)]
            made = after = between(arrived, last)
        short = at(1 - far + step, arrived, [after])
    return made, [value for pair in zip(last, short) for value in pair]


def block_adapters(pool, entries, requests, sources, slots):
    def pick(values, at):
        hit = at[:, None] == jnp.arange(values.shape[0], dtype=jnp.int32)[None]
        return jnp.sum(jnp.where(hit, values[None], 0), axis=1)

    entry = pick(entries, requests)
    fetch = jnp.clip(entry - pool, 0, slots.shape[0] - 1)
    adapter = pick(sources * pool + slots, fetch)
    return jnp.where(entry < pool, lax.axis_index("group") * pool + entry, adapter)


def per_device(
    tokens, kv_weight, a_pool, b_pool, request_entry, block_request, fetch_source, fetch_slot
):
    tensor = lax.axis_size("tensor")
    rows = tokens.shape[0]
    depth = tokens.shape[1]
    held = jnp.concatenate([a_pool, b_pool[:, :, :HEAD], b_pool[:, :, HEAD:]], axis=1)
    pools = lax.all_gather(held, "group", tiled=True)
    adapters = block_adapters(
        a_pool.shape[0], request_entry, block_request[0], fetch_source[:, 0], fetch_slot
    )

    def adapted(arrived, last):
        shrink = partial_shrink(adapters, tokens, pools, arrived)
        shrink, _ = lax.optimization_barrier((shrink, last))
        shrink = lax.all_to_all(shrink, "tensor", split_axis=0, concat_axis=0, tiled=True)
        shrink = shrink.reshape(tensor, rows // tensor, shrink.shape[1]).astype(jnp.float32)
        return jnp.sum(shrink, axis=0).astype(jnp.bfloat16)

    shrink, sums = ring_sum(tokens, kv_weight, adapted)
    shrink = jnp.broadcast_to(shrink[None], (tensor,) + shrink.shape).reshape(rows, -1)
    shrink = lax.all_to_all(shrink, "tensor", split_axis=0, concat_axis=0, tiled=True)
    base, lift = turn(adapters, sums, pools, pools.shape[1] - depth)
    return finish(base, shrink, lift)


def solution(mesh):
    placed = (
        P("group", "tensor"),
        P("tensor", None),
        P("group", "tensor", None),
        P("group", None, "tensor"),
        P("group"),
        P("group", None),
        P("group", None),
        P("group"),
    )
    return jax.shard_map(
        per_device, mesh=mesh, in_specs=placed, out_specs=P("tensor", "group"), check_vma=False
    )
```

```python
import functools

import jax
import jax.numpy as jnp
from jax import lax
from jax.experimental import pallas as pl
from jax.experimental.pallas import tpu as pltpu
from jax.sharding import PartitionSpec as P

HEAD = 128
TILE = 512
VMEM = 50 * 2**20
NT = (((1,), (1,)), ((), ()))


def product_kernel(arrived, owner_ref, tokens_ref, weight_ref, *refs):
    outs = refs[-6:-4]
    token_buf, weight_buf, token_sems, weight_sems = refs[-4:]
    columns = outs[0].shape[1]
    tiles = token_buf.shape[0]
    each = tiles // 2

    def token_copy(i):
        return pltpu.make_async_copy(
            tokens_ref.at[pl.ds(i * TILE, TILE)], token_buf.at[i], token_sems.at[i]
        )

    def weight_copy(which):
        at = pl.ds(pl.multiple_of(owner_ref[which] * columns, columns), columns)
        return pltpu.make_async_copy(
            weight_ref.at[:, at], weight_buf.at[which], weight_sems.at[which]
        )

    def fetch(i):
        which = i // each
        token_copy(i).start()
        if i % each == 0:
            weight_copy(which).start()

    ahead = 2
    for i in range(ahead):
        fetch(i)
    for i in range(tiles):
        which = i // each
        token_copy(i).wait()
        if i % each == 0:
            weight_copy(which).wait()
        if i + ahead < tiles:
            fetch(i + ahead)
        rows = slice(i % each * TILE, (i % each + 1) * TILE)
        total = jnp.dot(token_buf[i], weight_buf[which], preferred_element_type=jnp.float32)
        if arrived:
            total += refs[which][rows, :].astype(jnp.float32)
        outs[which][rows, :] = total.astype(outs[which].dtype)


def product(tokens, kv_weight, owners, columns, arrived=(), after=()):
    rows, depth = tokens.shape
    hbm = pl.BlockSpec(memory_space=pl.ANY)
    vmem = pl.BlockSpec(memory_space=pltpu.VMEM)
    return pl.pallas_call(
        functools.partial(product_kernel, len(arrived)),
        in_specs=[pl.BlockSpec(memory_space=pltpu.SMEM), hbm, hbm]
        + [vmem] * len(arrived)
        + [hbm] * len(after),
        out_specs=[vmem] * 2,
        out_shape=[jax.ShapeDtypeStruct((rows // 2, columns), jnp.bfloat16)] * 2,
        scratch_shapes=[
            pltpu.VMEM((rows // TILE, TILE, depth), jnp.bfloat16),
            pltpu.VMEM((2, depth, columns), jnp.bfloat16),
            pltpu.SemaphoreType.DMA((rows // TILE,)),
            pltpu.SemaphoreType.DMA((2,)),
        ],
        cost_estimate=pl.CostEstimate(
            flops=2 * rows * depth * columns,
            bytes_accessed=2 * (rows * depth + (2 * depth + rows) * columns),
            transcendentals=0,
        ),
        compiler_params=pltpu.CompilerParams(vmem_limit_bytes=VMEM),
        name="product",
    )(owners, tokens, kv_weight, *arrived, *after)


def shrink_kernel(
    adapter_ref, tokens_ref, pool_ref, first_ref, second_ref, out_ref, token_buf, factor_buf, sems
):
    del first_ref, second_ref
    blocks, tile, _ = token_buf.shape

    def copies(b):
        at = pl.ds(pl.multiple_of(b * tile, tile), tile)
        return (
            pltpu.make_async_copy(tokens_ref.at[at], token_buf.at[b], sems.at[b, 0]),
            pltpu.make_async_copy(
                pool_ref.at[adapter_ref[b]], factor_buf.at[b], sems.at[b, 1]
            ),
        )

    ahead = 6
    for b in range(ahead):
        for copy in copies(b):
            copy.start()
    for b in range(blocks):
        for copy in copies(b):
            copy.wait()
        if b + ahead < blocks:
            for copy in copies(b + ahead):
                copy.start()
        out_ref[b * tile : (b + 1) * tile, :] = jnp.dot(
            token_buf[b], factor_buf[b], preferred_element_type=jnp.float32
        ).astype(out_ref.dtype)


def partial_shrink(adapters, tokens, pools, after):
    blocks = adapters.shape[0]
    rows, depth = tokens.shape
    width = pools.shape[2]
    return pl.pallas_call(
        shrink_kernel,
        in_specs=[pl.BlockSpec(memory_space=pltpu.SMEM)]
        + [pl.BlockSpec(memory_space=pl.ANY)] * 4,
        out_specs=pl.BlockSpec(memory_space=pltpu.VMEM),
        out_shape=jax.ShapeDtypeStruct((rows, width), jnp.bfloat16),
        scratch_shapes=[
            pltpu.VMEM((blocks, rows // blocks, depth), jnp.bfloat16),
            pltpu.VMEM((blocks, depth, width), jnp.bfloat16),
            pltpu.SemaphoreType.DMA((blocks, 2)),
        ],
        cost_estimate=pl.CostEstimate(
            flops=2 * rows * depth * width,
            bytes_accessed=2 * (rows + blocks * width) * depth,
            transcendentals=0,
        ),
        compiler_params=pltpu.CompilerParams(vmem_limit_bytes=VMEM),
        name="partial_shrink",
    )(adapters, tokens, pools, *after)


def take_kernel(adapter_ref, pool_ref, after_ref, out_ref, sems):
    del after_ref

    def copy(b):
        return pltpu.make_async_copy(pool_ref.at[adapter_ref[b]], out_ref.at[b], sems.at[b])

    for b in range(out_ref.shape[0]):
        copy(b).start()
    for b in range(out_ref.shape[0]):
        copy(b).wait()


def take(adapters, pools, after):
    blocks = adapters.shape[0]
    return pl.pallas_call(
        take_kernel,
        in_specs=[pl.BlockSpec(memory_space=pltpu.SMEM)]
        + [pl.BlockSpec(memory_space=pl.ANY)] * 2,
        out_specs=pl.BlockSpec(memory_space=pltpu.VMEM),
        out_shape=jax.ShapeDtypeStruct((blocks,) + pools.shape[1:], pools.dtype),
        scratch_shapes=[pltpu.SemaphoreType.DMA((blocks,))],
        compiler_params=pltpu.CompilerParams(vmem_limit_bytes=60 * 2**20),
        name="take",
    )(adapters, pools, after)


def turn_kernel(*refs):
    sums, out_ref = refs[:4], refs[4]
    columns = out_ref.shape[0]
    half = out_ref.shape[1] // 2
    line = lax.broadcasted_iota(jnp.int32, (columns, columns), 0)
    lane = lax.broadcasted_iota(jnp.int32, (columns, columns), 1)
    eye = jnp.where(line == lane, 1.0, 0.0).astype(jnp.bfloat16)
    for which in range(2):
        for start in range(0, half, TILE):
            at = slice(start, start + TILE)
            total = add(sums[2 * which][at, :], sums[2 * which + 1][at, :])
            out_ref[:, which * half + start : which * half + start + TILE] = lax.dot_general(
                eye, total, NT, preferred_element_type=jnp.float32
            ).astype(out_ref.dtype)


def turn(sums):
    rows, columns = 2 * sums[0].shape[0], sums[0].shape[1]
    vmem = pl.BlockSpec(memory_space=pltpu.VMEM)
    return pl.pallas_call(
        turn_kernel,
        in_specs=[vmem] * 4,
        out_specs=vmem,
        out_shape=jax.ShapeDtypeStruct((columns, rows), jnp.bfloat16),
        cost_estimate=pl.CostEstimate(
            flops=2 * rows * columns * columns, bytes_accessed=6 * rows * columns, transcendentals=0
        ),
        compiler_params=pltpu.CompilerParams(vmem_limit_bytes=VMEM),
        name="turn",
    )(*sums)


def finish_kernel(base_ref, shrink_ref, lift_ref, out_ref):
    blocks, rank, _ = lift_ref.shape
    tile = base_ref.shape[1] // blocks
    for b in range(blocks):
        at = slice(b * tile, (b + 1) * tile)
        for kind in range(2):
            rows = slice(kind * HEAD, (kind + 1) * HEAD)
            ranks = slice(kind * rank, (kind + 1) * rank)
            delta = lax.dot_general(
                lift_ref[b, :, rows],
                shrink_ref[at, ranks],
                (((0,), (1,)), ((), ())),
                preferred_element_type=jnp.float32,
            )
            out_ref[rows, at] = (base_ref[rows, at].astype(jnp.float32) + delta).astype(
                out_ref.dtype
            )


def finish(base, shrink, lift):
    columns, rows = base.shape
    steps = 2
    step, lifts = rows // steps, lift.shape[0] // steps
    return pl.pallas_call(
        finish_kernel,
        grid=(steps,),
        in_specs=[
            pl.BlockSpec((columns, step), lambda i: (0, i)),
            pl.BlockSpec((step, shrink.shape[1]), lambda i: (i, 0)),
            pl.BlockSpec((lifts,) + lift.shape[1:], lambda i: (i, 0, 0)),
        ],
        out_specs=pl.BlockSpec((columns, step), lambda i: (0, i)),
        out_shape=jax.ShapeDtypeStruct((columns, rows), jnp.bfloat16),
        cost_estimate=pl.CostEstimate(
            flops=2 * rows * columns * HEAD, bytes_accessed=6 * rows * columns, transcendentals=0
        ),
        compiler_params=pltpu.CompilerParams(vmem_limit_bytes=VMEM),
        name="finish",
    )(base, shrink, lift)


def add(*terms):
    return sum(term.astype(jnp.float32) for term in terms).astype(jnp.bfloat16)


def ring_sum(tokens, kv_weight, between):
    count = lax.axis_size("tensor")
    me = lax.axis_index("tensor")
    far = count // 2

    def hop(value, way):
        return lax.ppermute(value, "tensor", [(i, (i + way) % count) for i in range(count)])

    ways = (1, -1)
    columns = kv_weight.shape[1] // count

    def at(shift, arrived=(), after=()):
        owners = (me + jnp.array([way * shift for way in ways], jnp.int32) + count) % count
        return product(tokens, kv_weight, owners, columns, arrived, after)

    long = at(far)
    short = at(1 - far, after=long[:1])
    for step in range(1, far):
        long = at(far - step, [hop(value, way) for value, way in zip(long, ways)], short[:1])
        arrived = [hop(value, -way) for value, way in zip(short, ways)]
        after = long[0]
        if step == far - 1:
            last = [hop(value, way) for value, way in zip(long, ways)]
            made = after = between(arrived, last)
        short = at(1 - far + step, arrived, [after])
    return made, [value for pair in zip(last, short) for value in pair]


def block_adapters(pool, entries, requests, sources, slots):
    def pick(values, at):
        hit = at[:, None] == jnp.arange(values.shape[0], dtype=jnp.int32)[None]
        return jnp.sum(jnp.where(hit, values[None], 0), axis=1)

    entry = pick(entries, requests)
    fetch = jnp.clip(entry - pool, 0, slots.shape[0] - 1)
    adapter = pick(sources * pool + slots, fetch)
    return jnp.where(entry < pool, lax.axis_index("group") * pool + entry, adapter)


def per_device(
    tokens, kv_weight, a_pool, b_pool, request_entry, block_request, fetch_source, fetch_slot
):
    tensor = lax.axis_size("tensor")
    rows = tokens.shape[0]
    pools_a = lax.all_gather(a_pool, "group", tiled=True)
    pools_b = lax.all_gather(b_pool, "group", tiled=True)
    adapters = block_adapters(
        a_pool.shape[0], request_entry, block_request[0], fetch_source[:, 0], fetch_slot
    )

    def adapted(arrived, last):
        shrink = partial_shrink(adapters, tokens, pools_a, arrived)
        shrink, _ = lax.optimization_barrier((shrink, last))
        shrink = lax.all_to_all(shrink, "tensor", split_axis=0, concat_axis=0, tiled=True)
        shrink = shrink.reshape(tensor, rows // tensor, shrink.shape[1]).astype(jnp.float32)
        return jnp.sum(shrink, axis=0).astype(jnp.bfloat16)

    shrink, sums = ring_sum(tokens, kv_weight, adapted)
    shrink = jnp.broadcast_to(shrink[None], (tensor,) + shrink.shape).reshape(rows, -1)
    shrink = lax.all_to_all(shrink, "tensor", split_axis=0, concat_axis=0, tiled=True)
    base = turn(sums)
    return finish(base, shrink, take(adapters, pools_b, base))


def solution(mesh):
    placed = (
        P("group", "tensor"),
        P("tensor", None),
        P("group", "tensor", None),
        P("group", None, "tensor"),
        P("group"),
        P("group", None),
        P("group", None),
        P("group"),
    )
    return jax.shard_map(
        per_device, mesh=mesh, in_specs=placed, out_specs=P("tensor", "group"), check_vma=False
    )
```

```python
import functools

import jax
import jax.numpy as jnp
from jax import lax
from jax.experimental import pallas as pl
from jax.experimental.pallas import tpu as pltpu
from jax.sharding import PartitionSpec as P

HEAD = 128
TILE = 512
VMEM = 50 * 2**20
NT = (((1,), (1,)), ((), ()))


def product_kernel(arrived, owner_ref, tokens_ref, weight_ref, *refs):
    outs = refs[-6:-4]
    token_buf, weight_buf, token_sems, weight_sems = refs[-4:]
    columns = outs[0].shape[1]
    tiles = token_buf.shape[0]
    each = tiles // 2

    def token_copy(i):
        return pltpu.make_async_copy(
            tokens_ref.at[pl.ds(i * TILE, TILE)], token_buf.at[i], token_sems.at[i]
        )

    def weight_copy(which):
        at = pl.ds(pl.multiple_of(owner_ref[which] * columns, columns), columns)
        return pltpu.make_async_copy(
            weight_ref.at[:, at], weight_buf.at[which], weight_sems.at[which]
        )

    def fetch(i):
        which = i // each
        token_copy(i).start()
        if i % each == 0:
            weight_copy(which).start()

    ahead = 2
    for i in range(ahead):
        fetch(i)
    for i in range(tiles):
        which = i // each
        token_copy(i).wait()
        if i % each == 0:
            weight_copy(which).wait()
        if i + ahead < tiles:
            fetch(i + ahead)
        rows = slice(i % each * TILE, (i % each + 1) * TILE)
        total = jnp.dot(token_buf[i], weight_buf[which], preferred_element_type=jnp.float32)
        if arrived:
            total += refs[which][rows, :].astype(jnp.float32)
        outs[which][rows, :] = total.astype(outs[which].dtype)


def product(tokens, kv_weight, owners, columns, arrived=(), after=()):
    rows, depth = tokens.shape
    hbm = pl.BlockSpec(memory_space=pl.ANY)
    vmem = pl.BlockSpec(memory_space=pltpu.VMEM)
    return pl.pallas_call(
        functools.partial(product_kernel, len(arrived)),
        in_specs=[pl.BlockSpec(memory_space=pltpu.SMEM), hbm, hbm]
        + [vmem] * len(arrived)
        + [hbm] * len(after),
        out_specs=[vmem] * 2,
        out_shape=[jax.ShapeDtypeStruct((rows // 2, columns), jnp.bfloat16)] * 2,
        scratch_shapes=[
            pltpu.VMEM((rows // TILE, TILE, depth), jnp.bfloat16),
            pltpu.VMEM((2, depth, columns), jnp.bfloat16),
            pltpu.SemaphoreType.DMA((rows // TILE,)),
            pltpu.SemaphoreType.DMA((2,)),
        ],
        cost_estimate=pl.CostEstimate(
            flops=2 * rows * depth * columns,
            bytes_accessed=2 * (rows * depth + (2 * depth + rows) * columns),
            transcendentals=0,
        ),
        compiler_params=pltpu.CompilerParams(vmem_limit_bytes=VMEM),
        name="product",
    )(owners, tokens, kv_weight, *arrived, *after)


def shrink_kernel(
    adapter_ref, tokens_ref, pool_ref, first_ref, second_ref, out_ref, token_buf, factor_buf, sems
):
    del first_ref, second_ref
    blocks, tile, _ = token_buf.shape

    def copies(b):
        at = pl.ds(pl.multiple_of(b * tile, tile), tile)
        return (
            pltpu.make_async_copy(tokens_ref.at[at], token_buf.at[b], sems.at[b, 0]),
            pltpu.make_async_copy(
                pool_ref.at[adapter_ref[b]], factor_buf.at[b], sems.at[b, 1]
            ),
        )

    ahead = 6
    for b in range(ahead):
        for copy in copies(b):
            copy.start()
    for b in range(blocks):
        for copy in copies(b):
            copy.wait()
        if b + ahead < blocks:
            for copy in copies(b + ahead):
                copy.start()
        out_ref[b * tile : (b + 1) * tile, :] = jnp.dot(
            token_buf[b], factor_buf[b], preferred_element_type=jnp.float32
        ).astype(out_ref.dtype)


def partial_shrink(adapters, tokens, pools, after):
    blocks = adapters.shape[0]
    rows, depth = tokens.shape
    width = pools.shape[2]
    return pl.pallas_call(
        shrink_kernel,
        in_specs=[pl.BlockSpec(memory_space=pltpu.SMEM)]
        + [pl.BlockSpec(memory_space=pl.ANY)] * 4,
        out_specs=pl.BlockSpec(memory_space=pltpu.VMEM),
        out_shape=jax.ShapeDtypeStruct((rows, width), jnp.bfloat16),
        scratch_shapes=[
            pltpu.VMEM((blocks, rows // blocks, depth), jnp.bfloat16),
            pltpu.VMEM((blocks, depth, width), jnp.bfloat16),
            pltpu.SemaphoreType.DMA((blocks, 2)),
        ],
        cost_estimate=pl.CostEstimate(
            flops=2 * rows * depth * width,
            bytes_accessed=2 * (rows + blocks * width) * depth,
            transcendentals=0,
        ),
        compiler_params=pltpu.CompilerParams(vmem_limit_bytes=VMEM),
        name="partial_shrink",
    )(adapters, tokens, pools, *after)


def turn_kernel(*refs):
    sums, out_ref = refs[:4], refs[4]
    columns = out_ref.shape[0]
    half = out_ref.shape[1] // 2
    line = lax.broadcasted_iota(jnp.int32, (columns, columns), 0)
    lane = lax.broadcasted_iota(jnp.int32, (columns, columns), 1)
    eye = jnp.where(line == lane, 1.0, 0.0).astype(jnp.bfloat16)
    for which in range(2):
        for start in range(0, half, TILE):
            at = slice(start, start + TILE)
            total = add(sums[2 * which][at, :], sums[2 * which + 1][at, :])
            out_ref[:, which * half + start : which * half + start + TILE] = lax.dot_general(
                eye, total, NT, preferred_element_type=jnp.float32
            ).astype(out_ref.dtype)


def turn(sums):
    rows, columns = 2 * sums[0].shape[0], sums[0].shape[1]
    vmem = pl.BlockSpec(memory_space=pltpu.VMEM)
    return pl.pallas_call(
        turn_kernel,
        in_specs=[vmem] * 4,
        out_specs=vmem,
        out_shape=jax.ShapeDtypeStruct((columns, rows), jnp.bfloat16),
        cost_estimate=pl.CostEstimate(
            flops=2 * rows * columns * columns, bytes_accessed=6 * rows * columns, transcendentals=0
        ),
        compiler_params=pltpu.CompilerParams(vmem_limit_bytes=VMEM),
        name="turn",
    )(*sums)


def finish_kernel(adapter_ref, base_ref, shrink_ref, pool_ref, out_ref):
    step = pl.program_id(0)
    tile = shrink_ref.shape[0] * pl.num_programs(0) // adapter_ref.shape[0]
    here = shrink_ref.shape[0] // tile
    rank = pool_ref.shape[1]
    for b in range(here):
        adapter = adapter_ref[step * here + b]
        at = slice(b * tile, (b + 1) * tile)
        for kind in range(2):
            rows = slice(kind * HEAD, (kind + 1) * HEAD)
            ranks = slice(kind * rank, (kind + 1) * rank)
            delta = lax.dot_general(
                pool_ref[adapter, :, rows],
                shrink_ref[at, ranks],
                (((0,), (1,)), ((), ())),
                preferred_element_type=jnp.float32,
            )
            out_ref[rows, at] = (base_ref[rows, at].astype(jnp.float32) + delta).astype(
                out_ref.dtype
            )


def finish(adapters, base, shrink, pools):
    columns, rows = base.shape
    steps = 2
    step = rows // steps
    return pl.pallas_call(
        finish_kernel,
        grid_spec=pltpu.PrefetchScalarGridSpec(
            num_scalar_prefetch=1,
            grid=(steps,),
            in_specs=[
                pl.BlockSpec((columns, step), lambda i, adapter: (0, i)),
                pl.BlockSpec((step, shrink.shape[1]), lambda i, adapter: (i, 0)),
                pl.BlockSpec(memory_space=pltpu.VMEM),
            ],
            out_specs=pl.BlockSpec((columns, step), lambda i, adapter: (0, i)),
        ),
        out_shape=jax.ShapeDtypeStruct((columns, rows), jnp.bfloat16),
        cost_estimate=pl.CostEstimate(
            flops=2 * rows * columns * HEAD, bytes_accessed=6 * rows * columns, transcendentals=0
        ),
        compiler_params=pltpu.CompilerParams(vmem_limit_bytes=24 * 2**20),
        name="finish",
    )(adapters, base, shrink, pools)


def add(*terms):
    return sum(term.astype(jnp.float32) for term in terms).astype(jnp.bfloat16)


def ring_sum(tokens, kv_weight, between):
    count = lax.axis_size("tensor")
    me = lax.axis_index("tensor")
    far = count // 2

    def hop(value, way):
        return lax.ppermute(value, "tensor", [(i, (i + way) % count) for i in range(count)])

    ways = (1, -1)
    columns = kv_weight.shape[1] // count

    def at(shift, arrived=(), after=()):
        owners = (me + jnp.array([way * shift for way in ways], jnp.int32) + count) % count
        return product(tokens, kv_weight, owners, columns, arrived, after)

    long = at(far)
    short = at(1 - far, after=long[:1])
    for step in range(1, far):
        long = at(far - step, [hop(value, way) for value, way in zip(long, ways)], short[:1])
        arrived = [hop(value, -way) for value, way in zip(short, ways)]
        after = long[0]
        if step == far - 1:
            last = [hop(value, way) for value, way in zip(long, ways)]
            made = after = between(arrived, last)
        short = at(1 - far + step, arrived, [after])
    return made, [value for pair in zip(last, short) for value in pair]


def block_adapters(pool, entries, requests, sources, slots):
    def pick(values, at):
        hit = at[:, None] == jnp.arange(values.shape[0], dtype=jnp.int32)[None]
        return jnp.sum(jnp.where(hit, values[None], 0), axis=1)

    entry = pick(entries, requests)
    fetch = jnp.clip(entry - pool, 0, slots.shape[0] - 1)
    adapter = pick(sources * pool + slots, fetch)
    return jnp.where(entry < pool, lax.axis_index("group") * pool + entry, adapter)


def per_device(
    tokens, kv_weight, a_pool, b_pool, request_entry, block_request, fetch_source, fetch_slot
):
    tensor = lax.axis_size("tensor")
    rows = tokens.shape[0]
    pools_a = lax.all_gather(a_pool, "group", tiled=True)
    pools_b = lax.all_gather(b_pool, "group", tiled=True)
    adapters = block_adapters(
        a_pool.shape[0], request_entry, block_request[0], fetch_source[:, 0], fetch_slot
    )

    def adapted(arrived, last):
        shrink = partial_shrink(adapters, tokens, pools_a, arrived)
        shrink, _ = lax.optimization_barrier((shrink, last))
        shrink = lax.all_to_all(shrink, "tensor", split_axis=0, concat_axis=0, tiled=True)
        shrink = shrink.reshape(tensor, rows // tensor, shrink.shape[1]).astype(jnp.float32)
        return jnp.sum(shrink, axis=0).astype(jnp.bfloat16)

    shrink, sums = ring_sum(tokens, kv_weight, adapted)
    shrink = jnp.broadcast_to(shrink[None], (tensor,) + shrink.shape).reshape(rows, -1)
    shrink = lax.all_to_all(shrink, "tensor", split_axis=0, concat_axis=0, tiled=True)
    return finish(adapters, turn(sums), shrink, pools_b)


def solution(mesh):
    placed = (
        P("group", "tensor"),
        P("tensor", None),
        P("group", "tensor", None),
        P("group", None, "tensor"),
        P("group"),
        P("group", None),
        P("group", None),
        P("group"),
    )
    return jax.shard_map(
        per_device, mesh=mesh, in_specs=placed, out_specs=P("tensor", "group"), check_vma=False
    )
```

```python
import functools

import jax
import jax.numpy as jnp
from jax import lax
from jax.experimental import pallas as pl
from jax.experimental.pallas import tpu as pltpu
from jax.sharding import PartitionSpec as P

HEAD = 128
CORES = 2
TILE = 512
VMEM = 50 * 2**20
NT = (((1,), (1,)), ((), ()))


def product_kernel(arrived, owner_ref, tokens_ref, weight_ref, *refs):
    outs = refs[-6:-4]
    token_buf, weight_buf, token_sems, weight_sems = refs[-4:]
    columns = outs[0].shape[1]
    tiles = token_buf.shape[0]
    each = tiles // 2

    def token_copy(i):
        return pltpu.make_async_copy(
            tokens_ref.at[pl.ds(i * TILE, TILE)], token_buf.at[i], token_sems.at[i]
        )

    def weight_copy(which):
        at = pl.ds(pl.multiple_of(owner_ref[which] * columns, columns), columns)
        return pltpu.make_async_copy(
            weight_ref.at[:, at], weight_buf.at[which], weight_sems.at[which]
        )

    def fetch(i):
        which = i // each
        token_copy(i).start()
        if i % each == 0:
            weight_copy(which).start()

    ahead = 2
    for i in range(ahead):
        fetch(i)
    for i in range(tiles):
        which = i // each
        token_copy(i).wait()
        if i % each == 0:
            weight_copy(which).wait()
        if i + ahead < tiles:
            fetch(i + ahead)
        rows = slice(i % each * TILE, (i % each + 1) * TILE)
        total = jnp.dot(token_buf[i], weight_buf[which], preferred_element_type=jnp.float32)
        if arrived:
            total += refs[which][rows, :].astype(jnp.float32)
        outs[which][rows, :] = total.astype(outs[which].dtype)


def product(tokens, kv_weight, owners, columns, arrived=(), after=()):
    rows, depth = tokens.shape
    hbm = pl.BlockSpec(memory_space=pl.ANY)
    vmem = pl.BlockSpec(memory_space=pltpu.VMEM)
    return pl.pallas_call(
        functools.partial(product_kernel, len(arrived)),
        in_specs=[pl.BlockSpec(memory_space=pltpu.SMEM), hbm, hbm]
        + [vmem] * len(arrived)
        + [hbm] * len(after),
        out_specs=[vmem] * 2,
        out_shape=[jax.ShapeDtypeStruct((rows // 2, columns), jnp.bfloat16)] * 2,
        scratch_shapes=[
            pltpu.VMEM((rows // TILE, TILE, depth), jnp.bfloat16),
            pltpu.VMEM((2, depth, columns), jnp.bfloat16),
            pltpu.SemaphoreType.DMA((rows // TILE,)),
            pltpu.SemaphoreType.DMA((2,)),
        ],
        cost_estimate=pl.CostEstimate(
            flops=2 * rows * depth * columns,
            bytes_accessed=2 * (rows * depth + (2 * depth + rows) * columns),
            transcendentals=0,
        ),
        compiler_params=pltpu.CompilerParams(vmem_limit_bytes=VMEM),
        name="product",
    )(owners, tokens, kv_weight, *arrived, *after)


def shrink_kernel(
    adapter_ref, tokens_ref, pool_ref, first_ref, second_ref, out_ref, token_buf, factor_buf, sems
):
    del first_ref, second_ref
    blocks, tile, _ = token_buf.shape

    def copies(b):
        at = pl.ds(pl.multiple_of(b * tile, tile), tile)
        return (
            pltpu.make_async_copy(tokens_ref.at[at], token_buf.at[b], sems.at[b, 0]),
            pltpu.make_async_copy(
                pool_ref.at[adapter_ref[b]], factor_buf.at[b], sems.at[b, 1]
            ),
        )

    ahead = 6
    for b in range(ahead):
        for copy in copies(b):
            copy.start()
    for b in range(blocks):
        for copy in copies(b):
            copy.wait()
        if b + ahead < blocks:
            for copy in copies(b + ahead):
                copy.start()
        out_ref[b * tile : (b + 1) * tile, :] = jnp.dot(
            token_buf[b], factor_buf[b], preferred_element_type=jnp.float32
        ).astype(out_ref.dtype)


def partial_shrink(adapters, tokens, pools, after):
    blocks = adapters.shape[0]
    rows, depth = tokens.shape
    width = pools.shape[2]
    return pl.pallas_call(
        shrink_kernel,
        in_specs=[pl.BlockSpec(memory_space=pltpu.SMEM)]
        + [pl.BlockSpec(memory_space=pl.ANY)] * 4,
        out_specs=pl.BlockSpec(memory_space=pltpu.VMEM),
        out_shape=jax.ShapeDtypeStruct((rows, width), jnp.bfloat16),
        scratch_shapes=[
            pltpu.VMEM((blocks, rows // blocks, depth), jnp.bfloat16),
            pltpu.VMEM((blocks, depth, width), jnp.bfloat16),
            pltpu.SemaphoreType.DMA((blocks, 2)),
        ],
        cost_estimate=pl.CostEstimate(
            flops=2 * rows * depth * width,
            bytes_accessed=2 * (rows + blocks * width) * depth,
            transcendentals=0,
        ),
        compiler_params=pltpu.CompilerParams(vmem_limit_bytes=VMEM),
        name="partial_shrink",
    )(adapters, tokens, pools, *after)


def turn_kernel(*refs):
    sums, out_ref = refs[:4], refs[4]
    columns = out_ref.shape[0]
    half = out_ref.shape[1] // 2
    line = lax.broadcasted_iota(jnp.int32, (columns, columns), 0)
    lane = lax.broadcasted_iota(jnp.int32, (columns, columns), 1)
    eye = jnp.where(line == lane, 1.0, 0.0).astype(jnp.bfloat16)
    for which in range(2):
        for start in range(0, half, TILE):
            at = slice(start, start + TILE)
            total = add(sums[2 * which][at, :], sums[2 * which + 1][at, :])
            out_ref[:, which * half + start : which * half + start + TILE] = lax.dot_general(
                eye, total, NT, preferred_element_type=jnp.float32
            ).astype(out_ref.dtype)


def turn(sums):
    rows, columns = 2 * sums[0].shape[0], sums[0].shape[1]
    vmem = pl.BlockSpec(memory_space=pltpu.VMEM)
    return pl.pallas_call(
        turn_kernel,
        in_specs=[vmem] * 4,
        out_specs=vmem,
        out_shape=jax.ShapeDtypeStruct((columns, rows), jnp.bfloat16),
        cost_estimate=pl.CostEstimate(
            flops=2 * rows * columns * columns, bytes_accessed=6 * rows * columns, transcendentals=0
        ),
        compiler_params=pltpu.CompilerParams(vmem_limit_bytes=VMEM),
        name="turn",
    )(*sums)


def finish_kernel(place_ref, base_ref, shrink_ref, own_ref, other_ref, out_ref):
    step = pl.program_id(0)
    tile = shrink_ref.shape[0] * pl.num_programs(0) // place_ref.shape[0]
    here = shrink_ref.shape[0] // tile
    count, rank, _ = own_ref.shape

    def write(b, table_ref, place):
        at = slice(b * tile, (b + 1) * tile)
        for kind in range(2):
            rows = slice(kind * HEAD, (kind + 1) * HEAD)
            ranks = slice(kind * rank, (kind + 1) * rank)
            delta = lax.dot_general(
                table_ref[place, :, rows],
                shrink_ref[at, ranks],
                (((0,), (1,)), ((), ())),
                preferred_element_type=jnp.float32,
            )
            out_ref[rows, at] = (base_ref[rows, at].astype(jnp.float32) + delta).astype(
                out_ref.dtype
            )

    for b in range(here):
        place = place_ref[step * here + b]
        pl.when(place < count)(functools.partial(write, b, own_ref, place))
        pl.when(place >= count)(functools.partial(write, b, other_ref, place - count))


def finish(places, base, shrink, own, other):
    columns, rows = base.shape
    steps = 2
    step = rows // steps
    return pl.pallas_call(
        finish_kernel,
        grid_spec=pltpu.PrefetchScalarGridSpec(
            num_scalar_prefetch=1,
            grid=(steps,),
            in_specs=[
                pl.BlockSpec((columns, step), lambda i, adapter: (0, i)),
                pl.BlockSpec((step, shrink.shape[1]), lambda i, adapter: (i, 0)),
                pl.BlockSpec(memory_space=pltpu.VMEM),
                pl.BlockSpec(memory_space=pltpu.VMEM),
            ],
            out_specs=pl.BlockSpec((columns, step), lambda i, adapter: (0, i)),
        ),
        out_shape=jax.ShapeDtypeStruct((columns, rows), jnp.bfloat16),
        cost_estimate=pl.CostEstimate(
            flops=2 * rows * columns * HEAD, bytes_accessed=6 * rows * columns, transcendentals=0
        ),
        compiler_params=pltpu.CompilerParams(vmem_limit_bytes=24 * 2**20),
        name="finish",
    )(places, base, shrink, own, other)


def add(*terms):
    return sum(term.astype(jnp.float32) for term in terms).astype(jnp.bfloat16)


def ring_sum(tokens, kv_weight, between):
    count = lax.axis_size("tensor")
    me = lax.axis_index("tensor")
    far = count // 2

    def hop(value, way):
        return lax.ppermute(value, "tensor", [(i, (i + way) % count) for i in range(count)])

    ways = (1, -1)
    columns = kv_weight.shape[1] // count

    def at(shift, arrived=(), after=()):
        owners = (me + jnp.array([way * shift for way in ways], jnp.int32) + count) % count
        return product(tokens, kv_weight, owners, columns, arrived, after)

    long = at(far)
    short = at(1 - far, after=long[:1])
    for step in range(1, far):
        long = at(far - step, [hop(value, way) for value, way in zip(long, ways)], short[:1])
        arrived = [hop(value, -way) for value, way in zip(short, ways)]
        after = long[0]
        if step == far - 1:
            last = [hop(value, way) for value, way in zip(long, ways)]
            made = after = between(arrived, last)
        short = at(1 - far + step, arrived, [after])
    return made, [value for pair in zip(last, short) for value in pair]


def block_adapters(pool, entries, requests, sources, slots):
    def pick(values, at):
        hit = at[:, None] == jnp.arange(values.shape[0], dtype=jnp.int32)[None]
        return jnp.sum(jnp.where(hit, values[None], 0), axis=1)

    entry = pick(entries, requests)
    fetch = jnp.clip(entry - pool, 0, slots.shape[0] - 1)
    adapter = pick(sources * pool + slots, fetch)
    return jnp.where(entry < pool, lax.axis_index("group") * pool + entry, adapter)


def per_device(
    tokens, kv_weight, a_pool, b_pool, request_entry, block_request, fetch_source, fetch_slot
):
    tensor = lax.axis_size("tensor")
    rows = tokens.shape[0]
    pools_a = lax.all_gather(a_pool, "group", tiled=True)
    groups = lax.axis_size("group")
    same = [list(range(core, groups, CORES)) for core in range(CORES)]
    own_b = lax.all_gather(b_pool, "group", axis_index_groups=same, tiled=True)
    other_b = lax.ppermute(own_b, "group", [(i, i ^ 1) for i in range(groups)])
    adapters = block_adapters(
        a_pool.shape[0], request_entry, block_request[0], fetch_source[:, 0], fetch_slot
    )

    def adapted(arrived, last):
        shrink = partial_shrink(adapters, tokens, pools_a, arrived)
        shrink, _ = lax.optimization_barrier((shrink, last))
        shrink = lax.all_to_all(shrink, "tensor", split_axis=0, concat_axis=0, tiled=True)
        shrink = shrink.reshape(tensor, rows // tensor, shrink.shape[1]).astype(jnp.float32)
        return jnp.sum(shrink, axis=0).astype(jnp.bfloat16)

    shrink, sums = ring_sum(tokens, kv_weight, adapted)
    shrink = jnp.broadcast_to(shrink[None], (tensor,) + shrink.shape).reshape(rows, -1)
    shrink = lax.all_to_all(shrink, "tensor", split_axis=0, concat_axis=0, tiled=True)
    pool = b_pool.shape[0]
    group = adapters // pool
    places = group // CORES * pool + adapters % pool
    far = group % CORES != lax.axis_index("group") % CORES
    places = jnp.where(far, places + own_b.shape[0], places)
    return finish(places, turn(sums), shrink, own_b, other_b)


def solution(mesh):
    placed = (
        P("group", "tensor"),
        P("tensor", None),
        P("group", "tensor", None),
        P("group", None, "tensor"),
        P("group"),
        P("group", None),
        P("group", None),
        P("group"),
    )
    return jax.shard_map(
        per_device, mesh=mesh, in_specs=placed, out_specs=P("tensor", "group"), check_vma=False
    )
```
